32 devices in a mesh: grp: 2 (over x), wide: 16 (over z, y, core).
Axes of the slice: x: 2, y: 2, z: 4, core: 2. Of those that a mesh axis runs over, the one named last changes fastest.
Arguments:
- query_maps: bfloat16 [4096, 1024], P(('grp', 'wide')), parts along dimension 0
- source_maps: bfloat16 [4096, 1024], P(('grp', 'wide')), parts along dimension 0
- hubs: int32 [8], P('grp'), parts along dimension 0, may hold values from 0 to 15, as said below
- pick: int32 [32, 2], P(('grp', 'wide')), parts along dimension 0, may hold values from 0 to 3, all different within a row
- weight_first: bfloat16 [16, 1, 3, 3, 3, 3], replicated, may hold values from -0.625 to 0.625
- bias_first: float32 [16], replicated, may hold values from -0.6 to 0.6
- weight_second: bfloat16 [1, 16, 3, 3, 3, 3], replicated, may hold values from -0.15625 to 0.15625
- bias_second: float32 [1], replicated, may hold values from 0 to 0.2
Outputs:
- consensus: float32 [32, 2, 128, 128], P(('grp', 'wide')), parts along dimension 0
The draws below stay inside these ranges and needn't reach their ends.
There are 2 independent parts, one for each index of `grp`. The reference program is written for one: setup_inputs(seed, part) draws one part's arguments, and reference() takes and returns one part's arrays. A program takes and returns all parts, laid end to end along the dimension named above; an argument that names none is the same for every part. Nothing has to cross between parts.
Inputs may be any that keep to these rules, and one draw needn't show every extreme that they name: `hubs`: distinct photo indices of the batch.
All inputs are finite; a program needn't handle non-finite values.
Results may differ from the reference program's by a relative error of at most 0.0063.
Values may be sent and summed in bfloat16 or wider, within the bound.
A program may use at most 64 MiB of HBM per device.

```python
import math
import jax
import jax.numpy as jnp
from jax import lax

C = 1024
HQ = 4
WQ = 32
HID = 16
HUBS = 4
CELLS = 128
ROWS = 2048
N_WIDE = 16


def row_features(key, salt):
    book_key = jax.random.fold_in(key, 5)
    own_key = jax.random.fold_in(key, salt)
    code_key, noise_key, scale_key = jax.random.split(own_key, 3)
    book = jax.random.normal(book_key, (16, C), jnp.float32)
    codes = jax.random.randint(code_key, (ROWS,), 0, 16)
    planted = jnp.take(book, codes, axis=0)
    noise = jax.random.normal(noise_key, (ROWS, C), jnp.float32)
    base = 0.8 * planted + 0.6 * noise
    scales = jnp.exp(jax.random.uniform(scale_key, (ROWS, 1), jnp.float32, 0.0, math.log(10.0)))
    return (base * scales).astype(jnp.bfloat16)


def draw_query_maps(key, part):
    return row_features(key, 11)


def draw_source_maps(key, part):
    return row_features(key, 23)


def draw_hubs(key, part):
    inner_key = jax.random.fold_in(key, 37)
    order_key = jax.random.fold_in(key, 41)
    middle = 1 + jax.random.permutation(inner_key, N_WIDE - 2)[:HUBS - 2]
    ends = jnp.array([0, N_WIDE - 1], dtype=jnp.int32)
    values = jnp.concatenate([ends, middle.astype(jnp.int32)])
    return jax.random.permutation(order_key, values).astype(jnp.int32)


def distinct(key, rows, count, top, lift):
    sequence = jax.random.permutation(jax.random.fold_in(key, 1), count)
    favour = sequence
    for power in range(3):
        favour = favour * favour // count
    favour = favour * lift // count
    lots = jax.random.randint(jax.random.fold_in(key, 2), (rows, count), 0, 4096) + favour
    sure = jax.random.permutation(jax.random.fold_in(key, 3), rows)[jnp.arange(count) % rows]
    lots = jnp.where(jnp.arange(rows)[:, None] == sure[None, :], 1 << 14, lots)
    priority = lots * count + jnp.arange(count)
    return lax.top_k(priority.astype(jnp.int32), top)[1].astype(jnp.int32)


def centred(key, extent, deviation, most, kind=jnp.bfloat16):
    values = deviation * jax.random.normal(key, extent, jnp.float32)
    return jnp.clip(values, min=-most, max=most).astype(kind)


def setup_inputs(seed: int = 0, part: int = 0) -> dict:
    splits = jax.random.split(jax.random.key(seed), 9)
    part_keys = jax.random.split(jax.random.fold_in(splits[8], part), 9)
    query_maps = draw_query_maps(jax.random.fold_in(jax.random.fold_in(splits[8], part), 71), part)
    source_maps = draw_source_maps(jax.random.fold_in(jax.random.fold_in(splits[8], part), 71), part)
    hubs = draw_hubs(jax.random.fold_in(jax.random.fold_in(splits[8], part), 71), part)
    pick = distinct(part_keys[3], N_WIDE, HUBS, 2, 8192)
    weight_first = centred(splits[4], (HID, 1, 3, 3, 3, 3), 81 ** -0.5, 0.625)
    bias_first = centred(splits[5], (HID,), 0.2, 0.6, jnp.float32)
    weight_second = centred(splits[6], (1, HID, 3, 3, 3, 3), (81 * HID) ** -0.5, 0.15625)
    bias_second = jnp.clip(jax.random.uniform(splits[7], (1,), jnp.float32, 0.0, 0.2), 0.0, 0.2)
    return dict(query_maps=query_maps, source_maps=source_maps, hubs=hubs, pick=pick, weight_first=weight_first, bias_first=bias_first, weight_second=weight_second, bias_second=bias_second)


def conv_volume(volume, kernel):
    padded = jnp.pad(volume, ((1, 1), (0, 0), (0, 0), (0, 0), (0, 0)))
    height = volume.shape[0]
    result = None
    for offset in range(3):
        term = lax.conv_general_dilated(padded[offset:offset + height], kernel[:, :, offset], (1, 1, 1), [(1, 1), (1, 1), (1, 1)], preferred_element_type=jnp.float32)
        result = term if result is None else result + term
    return result

def consensus_net(matrix, weight_first, bias_first, weight_second, bias_second):
    volume = matrix.reshape(HQ, WQ, HQ, WQ)[:, None]
    preact = conv_volume(volume, weight_first) + bias_first[None, :, None, None, None]
    hidden = jax.nn.relu(preact).astype(jnp.bfloat16)
    result = jax.nn.relu(conv_volume(hidden, weight_second) + bias_second[None, :, None, None, None])
    return result.reshape(CELLS, CELLS)

def scaled_corr(query, sources):
    query_f = query.astype(jnp.float32)
    sources_f = sources.astype(jnp.float32)
    query_rms = jnp.sqrt(lax.optimization_barrier(jnp.mean(query_f * query_f, axis=-1)) + 1e-06)
    source_rms = jnp.sqrt(lax.optimization_barrier(jnp.mean(sources_f * sources_f, axis=-1)) + 1e-06)
    inner = jnp.einsum('ac,jbc->jab', query_f, sources_f, precision=lax.Precision.HIGHEST)
    scale = jnp.sqrt(jnp.float32(C))
    return (inner / (scale * query_rms[None, :, None] * source_rms[:, None, :])).astype(jnp.bfloat16)

def reference(query_maps, source_maps, hubs, pick, weight_first, bias_first, weight_second, bias_second):
    queries = query_maps.reshape(N_WIDE, CELLS, C)
    sources = source_maps.reshape(N_WIDE, CELLS, C)
    owners = hubs[pick]

    def position(index):
        chosen = sources[owners[index]]
        correlation = scaled_corr(queries[index], chosen)
        filtered = []
        for pair in range(2):
            forward = consensus_net(correlation[pair], weight_first, bias_first, weight_second, bias_second)
            backward = consensus_net(correlation[pair].T, weight_first, bias_first, weight_second, bias_second)
            filtered.append(forward + backward.T)
        return jnp.stack(filtered)
    return lax.map(position, jnp.arange(N_WIDE, dtype=jnp.int32))
```

```python
import functools

import jax
import jax.numpy as jnp
from jax import lax
from jax.experimental import pallas as pl
from jax.experimental.pallas import tpu as pltpu
from jax.sharding import PartitionSpec as P

HQ = 4
WQ = 32
CELLS = HQ * WQ
HID = 16
TAPS = 9
NETS = 4
ROWS16 = 16
OFFSETS = [(i, j) for i in (-1, 0, 1) for j in (-1, 0, 1)]


def iota(shape, dim):
    return lax.broadcasted_iota(jnp.int32, shape, dim)


def tap_vectors(taps_ref, v_ref):
    row, lane = iota((128, CELLS), 0), iota((128, CELLS), 1)
    place = jnp.zeros((128, CELLS), jnp.bool_)
    for t, (i, j) in enumerate(OFFSETS):
        place |= (row == t) & (lane == (-(WQ * i + j)) % CELLS)
    spread = jnp.where(place, 1.0, 0.0).astype(jnp.bfloat16)
    v_ref[...] = jnp.dot(taps_ref[...], spread, preferred_element_type=jnp.float32)


def band_mask():
    cin, cout = iota((CELLS, CELLS), 0), iota((CELLS, CELLS), 1)
    rows = jnp.abs((cin >> 5) - (cout >> 5)) <= 1
    columns = jnp.abs((cin & (WQ - 1)) - (cout & (WQ - 1))) <= 1
    return jnp.where(rows & columns, 1.0, 0.0)


def band(v_ref, index, mask):
    line = jnp.broadcast_to(v_ref[pl.ds(index, 1), :], (CELLS, CELLS))
    return (pltpu.roll(line, 0, 1, stride=1, stride_axis=0) * mask).astype(jnp.bfloat16)


def build_first(v_ref, w_ref):
    mask = band_mask()

    def body(o, _):
        for d in range(TAPS):
            w_ref[pl.ds(d * CELLS, CELLS), pl.ds(pl.multiple_of(o * CELLS, CELLS), CELLS)] = band(
                v_ref, o * TAPS + d, mask
            )
        return 0

    lax.fori_loop(0, HID, body, 0)


def build_second(v_ref, w_ref):
    mask = band_mask()

    def body(o, _):
        for d in range(TAPS):
            w_ref[pl.ds(pl.multiple_of(o * CELLS, CELLS), CELLS), pl.ds(d * CELLS, CELLS)] = band(
                v_ref, HID * TAPS + o * TAPS + d, mask
            )
        return 0

    lax.fori_loop(0, HID, body, 0)


def column_shift(value, j):
    if j == 0:
        return value
    rows = value.shape[0]
    column = iota(value.shape, 0) & (WQ - 1)
    moved = pltpu.roll(value, (-j) % rows, 0)
    inside = column < WQ - 1 if j > 0 else column > 0
    return jnp.where(inside, moved, 0.0)


def row_pieces(i):
    if i == 0:
        return (0, CELLS), (0, CELLS), None
    if i < 0:
        return (WQ, CELLS), (0, CELLS - WQ), (0, WQ)
    return (0, CELLS - WQ), (WQ, CELLS), (CELLS - WQ, CELLS)


def correlate(q_ref, chosen, pair):
    query, source = q_ref[...], chosen[pair]
    channels = query.shape[1]
    qf, sf = query.astype(jnp.float32), source.astype(jnp.float32)
    rq = jnp.sqrt(jnp.sum(qf * qf, axis=1, keepdims=True) / channels + 1e-06)
    rs = jnp.sqrt(jnp.sum(sf * sf, axis=1, keepdims=True) / channels + 1e-06)
    rs = jnp.broadcast_to(rs, (CELLS, CELLS)).T
    inner = lax.dot_general(
        query, source, (((1,), (1,)), ((), ())), preferred_element_type=jnp.float32
    )
    corr = inner / (jnp.sqrt(jnp.float32(channels)) * rq * rs)
    return corr.astype(jnp.bfloat16).astype(jnp.float32)


def fill_shifted(x_ref, net, matrix):
    base = net * CELLS
    for jn, j in enumerate((-1, 0, 1)):
        moved = column_shift(matrix, j).astype(jnp.bfloat16)
        for im, i in enumerate((-1, 0, 1)):
            d = im * 3 + jn
            (w0, w1), (r0, r1), gap = row_pieces(i)
            x_ref[base + w0 : base + w1, d * CELLS : (d + 1) * CELLS] = moved[r0:r1]
            if gap is not None:
                x_ref[base + gap[0] : base + gap[1], d * CELLS : (d + 1) * CELLS] = jnp.zeros(
                    (WQ, CELLS), jnp.bfloat16
                )


def first_conv(x_ref, w_ref, b_ref, h_ref):
    def body(c, _):
        at = pl.ds(pl.multiple_of(c * 256, 256), 256)
        acc = jnp.dot(x_ref[...], w_ref[:, at], preferred_element_type=jnp.float32)
        lane = iota((1, 256), 1)
        bias = jnp.where(lane < CELLS, b_ref[2 * c], b_ref[2 * c + 1])
        h_ref[:, at] = jnp.maximum(acc + bias, 0.0).astype(jnp.bfloat16)
        return 0

    lax.fori_loop(0, HID * CELLS // 256, body, 0)


def second_conv(h_ref, w_ref, y_ref):
    def body(c, _):
        at = pl.ds(pl.multiple_of(c * 256, 256), 256)
        y_ref[:, at] = jnp.dot(h_ref[...], w_ref[:, at], preferred_element_type=jnp.float32)
        return 0

    lax.fori_loop(0, TAPS * CELLS // 256, body, 0)
    rest = TAPS * CELLS // 256 * 256
    y_ref[:, rest:] = jnp.dot(h_ref[...], w_ref[:, rest:], preferred_element_type=jnp.float32)


def combine(y_ref, net, bias):
    base = net * CELLS
    total = None
    for jn, j in enumerate((-1, 0, 1)):
        part = []
        for r in range(HQ):
            piece = None
            for im, i in enumerate((-1, 0, 1)):
                if 0 <= r + i < HQ:
                    d = im * 3 + jn
                    start = base + (r + i) * WQ
                    term = y_ref[start : start + WQ, d * CELLS : (d + 1) * CELLS]
                    piece = term if piece is None else piece + term
            part.append(piece)
        term = column_shift(jnp.concatenate(part, axis=0), j)
        total = term if total is None else total + term
    return jnp.maximum(total + bias, 0.0)


def kernel(
    n, q_ref, s_ref, hubs_ref, pick_ref, taps_ref, b1_ref, b2_ref, out_ref,
    stage, mine, owners, outbox, chosen, v, w1, w2, x, h, y,
    send1, recv1, sendo, recvo, send2, recv2, local,
):
    me = lax.axis_index("wide")
    across = n // (CELLS // ROWS16)
    width = s_ref.shape[1] // across

    def piece(index):
        return (
            pl.ds(pl.multiple_of((index // across) * ROWS16, ROWS16), ROWS16),
            pl.ds(pl.multiple_of((index % across) * width, width), width),
        )

    def peers(body):
        def step(s, _):
            body(lax.rem(me + s, n))
            return 0

        lax.fori_loop(1, n, step, 0)

    barrier = pltpu.get_barrier_semaphore()
    peers(lambda p: pl.semaphore_signal(
        barrier, inc=1, device_id={"wide": p}, device_id_type=pl.DeviceIdType.MESH))

    row = iota((8, 128), 0)
    mine[...] = jnp.where(row < 4, hubs_ref[pick_ref[0, 0]], hubs_ref[pick_ref[0, 1]])
    own_rows, own_columns = piece(me)
    keep = pltpu.make_async_copy(s_ref.at[own_rows, own_columns], stage.at[me], local.at[0])
    keep.start()
    pl.semaphore_wait(barrier, n - 1)

    def scatter(p, slot):
        rows, columns = piece(p)
        return pltpu.make_async_remote_copy(
            src_ref=s_ref.at[rows, columns], dst_ref=stage.at[slot],
            send_sem=send1.at[p], recv_sem=recv1.at[slot],
            device_id={"wide": p}, device_id_type=pl.DeviceIdType.MESH)

    def tell(p, slot):
        return pltpu.make_async_remote_copy(
            src_ref=mine, dst_ref=owners.at[slot],
            send_sem=sendo.at[p], recv_sem=recvo.at[slot],
            device_id={"wide": p}, device_id_type=pl.DeviceIdType.MESH)

    def deliver(p, slot):
        rows, columns = piece(slot)
        return pltpu.make_async_remote_copy(
            src_ref=outbox.at[p], dst_ref=chosen.at[:, rows, columns],
            send_sem=send2.at[p], recv_sem=recv2.at[slot],
            device_id={"wide": p}, device_id_type=pl.DeviceIdType.MESH)

    def start_first(p):
        tell(p, me).start()
        scatter(p, me).start()

    peers(start_first)
    owners[me] = mine[...]
    tap_vectors(taps_ref, v)
    build_first(v, w1)
    keep.wait()

    def wait_first(p):
        tell(p, p).wait_recv()
        scatter(p, p).wait_recv()

    peers(wait_first)

    def pack(p):
        outbox[p, 0] = stage[owners[p, 0, 0]]
        outbox[p, 1] = stage[owners[p, 4, 0]]

    def send_second(p):
        pack(p)
        deliver(p, me).start()

    peers(send_second)
    pack(me)
    stay = pltpu.make_async_copy(
        outbox.at[me], chosen.at[:, own_rows, own_columns], local.at[1])
    stay.start()
    build_second(v, w2)
    stay.wait()
    peers(lambda p: deliver(p, p).wait_recv())

    for pair in range(2):
        corr = correlate(q_ref, chosen, pair)
        fill_shifted(x, pair, corr)
        fill_shifted(x, 2 + pair, corr.T)
    first_conv(x, w1, b1_ref, h)
    second_conv(h, w2, y)
    for pair in range(2):
        forward = combine(y, pair, b2_ref[0])
        backward = combine(y, 2 + pair, b2_ref[0])
        out_ref[0, pair] = forward + backward.T

    def wait_sent(p):
        tell(p, me).wait_send()
        scatter(p, me).wait_send()
        deliver(p, me).wait_send()

    peers(wait_sent)


def per_device(
    n, query_maps, source_maps, hubs, pick, weight_first, bias_first, weight_second, bias_second
):
    cells, channels = source_maps.shape
    taps = jnp.concatenate(
        [weight_first.reshape(HID * TAPS, TAPS), weight_second.reshape(HID * TAPS, TAPS)], axis=0
    )
    taps = jnp.pad(taps, ((0, 0), (0, 128 - TAPS)))
    width = channels // (n // (cells // ROWS16))
    vmem = pl.BlockSpec(memory_space=pltpu.VMEM)
    smem = pl.BlockSpec(memory_space=pltpu.SMEM)
    return pl.pallas_call(
        functools.partial(kernel, n),
        out_shape=jax.ShapeDtypeStruct((1, 2, cells, cells), jnp.float32),
        in_specs=[vmem, pl.BlockSpec(memory_space=pl.ANY), smem, smem, vmem, smem, smem],
        out_specs=vmem,
        scratch_shapes=[
            pltpu.VMEM((n, ROWS16, width), jnp.bfloat16),
            pltpu.VMEM((8, 128), jnp.int32),
            pltpu.VMEM((n, 8, 128), jnp.int32),
            pltpu.VMEM((n, 2, ROWS16, width), jnp.bfloat16),
            pltpu.VMEM((2, cells, channels), jnp.bfloat16),
            pltpu.VMEM((2 * HID * TAPS, CELLS), jnp.float32),
            pltpu.VMEM((TAPS * CELLS, HID * CELLS), jnp.bfloat16),
            pltpu.VMEM((HID * CELLS, TAPS * CELLS), jnp.bfloat16),
            pltpu.VMEM((NETS * CELLS, TAPS * CELLS), jnp.bfloat16),
            pltpu.VMEM((NETS * CELLS, HID * CELLS), jnp.bfloat16),
            pltpu.VMEM((NETS * CELLS, TAPS * CELLS), jnp.float32),
        ]
        + [pltpu.SemaphoreType.DMA((n,))] * 6
        + [pltpu.SemaphoreType.DMA((2,))],
        compiler_params=pltpu.CompilerParams(
            collective_id=0, has_side_effects=True, vmem_limit_bytes=40 * 1024 * 1024
        ),
        name="consensus",
    )(query_maps, source_maps, hubs, pick, taps, bias_first, bias_second)


def solution(mesh):
    return jax.shard_map(
        functools.partial(per_device, mesh.shape["wide"]),
        mesh=mesh,
        in_specs=(
            P(("grp", "wide"), None),
            P(("grp", "wide"), None),
            P("grp"),
            P(("grp", "wide"), None),
            P(),
            P(),
            P(),
            P(),
        ),
        out_specs=P(("grp", "wide"), None, None, None),
        check_vma=False,
    )
```
